32 devices in a mesh: grp: 2 (over y), row: 4 (over z), col: 2 (over x), rep: 2 (over core).
Axes of the slice: x: 2, y: 2, z: 4, core: 2. Of those that a mesh axis runs over, the one named last changes fastest.
Arguments:
- integrals: bfloat16 [256, 512, 512], P(('grp', 'col'), 'row', 'rep'), parts along dimension 0, may hold values from -6 to 6
- occ_density: bfloat16 [1024, 512], P('grp', 'rep'), parts along dimension 0, may hold values from -0.25 to 0.25
- virt_density: bfloat16 [1024, 512], P('grp'), parts along dimension 0, may hold values from -0.25 to 0.25
- pair_mask: int32 [8, 4], P('grp'), parts along dimension 0, may hold values 0 or 1
- aux_mask: int32 [2, 4], P('grp'), parts along dimension 0, may hold values 0 or 1
Outputs:
- response: float32 [256, 128], P(('grp', 'row', 'rep'), 'col'), parts along dimension 0
The draws below stay inside these ranges and needn't reach their ends.
There are 2 independent parts, one for each index of `grp`. The reference program is written for one: setup_inputs(seed, part) draws one part's arguments, and reference() takes and returns one part's arrays. A program takes and returns all parts, laid end to end along the dimension named above; each array names one. Nothing has to cross between parts.
All inputs are finite; a program needn't handle non-finite values.
Results may differ from the reference program's by a relative error of at most 0.004.
Values may be sent and summed in bfloat16 or wider, within the bound.
A program may use at most 64 MiB of HBM per device.

```python
import jax
import jax.numpy as jnp
from jax import lax

BLOCK = 128
RI_ATOM = 128
AO_BLOCKS = 4
NAO = 512
NRI = 128
RI_BLOCKS = 1


def plant(result, stream_key, low, high):
    extent = result.shape
    spot = [jax.random.randint(jax.random.fold_in(stream_key, axis), (), 0, extent[axis]) for axis in range(len(extent))]
    result = result.at[tuple(spot)].set(low)
    longest = extent.index(max(extent))
    spot[longest] = (spot[longest] + 1) % extent[longest]
    return result.at[tuple(spot)].set(high)


def steps_of(key, dims, split, smallest, high):
    level = 1.0
    for position, parts in split:
        heights = jax.random.uniform(jax.random.fold_in(jax.random.fold_in(key, 6), position), (parts,), jnp.float32, smallest / len(split), high / len(split))
        level = level * jnp.repeat(jnp.exp(heights), dims[position] // parts).reshape((-1,) + (1,) * (len(dims) - 1 - position))
    return level


def bell_draw(rng, dims, scale, limit, shards=(), held_as=jnp.bfloat16):
    level = steps_of(rng, dims, shards, -0.22, 0.18) if shards else 1.0
    drawn = jax.random.normal(rng, dims, jnp.float32) * scale * level
    return jnp.minimum(jnp.maximum(drawn, -limit), limit).astype(held_as)


def setup_inputs(seed: int = 0, part: int = 0) -> dict:
    streams_of = jax.random.split(jax.random.key(seed), 6)
    part_splits = jax.random.split(jax.random.fold_in(streams_of[5], part), 6)
    return {
        "integrals": bell_draw(part_splits[0], (NRI, NAO, NAO), 1.0, 6.0, ((0, 2), (1, 4), (2, 2))),
        "occ_density": bell_draw(part_splits[1], (NAO, NAO), NAO ** -0.5, 0.25, ((1, 2),)),
        "virt_density": bell_draw(part_splits[2], (NAO, NAO), NAO ** -0.5, 0.25),
        "pair_mask": plant((jax.random.randint(part_splits[3], (AO_BLOCKS, AO_BLOCKS), 0, 3) < 2).astype(jnp.int32), jax.random.fold_in(part_splits[3], 1), 0, 1),
        "aux_mask": plant((jax.random.randint(part_splits[4], (RI_BLOCKS, AO_BLOCKS), 0, 3) < 2).astype(jnp.int32), jax.random.fold_in(part_splits[4], 1), 0, 1),
    }


def reference(integrals, occ_density, virt_density, pair_mask, aux_mask):
    pair_full = jnp.repeat(jnp.repeat(pair_mask, BLOCK, axis=0), BLOCK, axis=1)
    aux_full = jnp.repeat(jnp.repeat(aux_mask, RI_ATOM, axis=0), BLOCK, axis=1)
    keep_mask = (aux_full[:, :, None] * jnp.transpose(pair_full)[None, :, :]).astype(jnp.bfloat16)
    masked = integrals * keep_mask
    occ_side = jnp.dot(masked.reshape(NRI * NAO, NAO), occ_density, preferred_element_type=jnp.float32)
    occ_side = occ_side.astype(jnp.bfloat16).reshape(NRI, NAO * NAO)
    virt_turned = jnp.transpose(virt_density)

    def one_virt(slab):
        return jnp.dot(virt_turned, slab, preferred_element_type=jnp.float32).astype(jnp.bfloat16)

    virt_side = lax.map(one_virt, masked).reshape(NRI, NAO * NAO)
    product = jnp.dot(occ_side, jnp.transpose(virt_side), preferred_element_type=jnp.float32)
    return product * (-2.0 / NAO)
```

```python
import functools

import jax
import jax.numpy as jnp
from jax import lax
from jax.experimental import pallas as pl
from jax.experimental.pallas import tpu as pltpu
from jax.sharding import PartitionSpec as P

BLOCK = 128
RI_ATOM = 128
NAO = 512
MESH = pl.DeviceIdType.MESH
F32 = jnp.float32
BF16 = jnp.bfloat16
GROUP = 16
STRIP = 64


def one_hot_blocks(first, count, width, groups):
    places = (first + jnp.arange(count, dtype=jnp.int32)) // width
    return (places[:, None] == jnp.arange(groups, dtype=jnp.int32)[None, :]).astype(F32)


def kernel(rows, m_ref, occ_ref, virt_ref, out_ref, sib, relaid, turned, occ_own, occ_far, back,
           total, parts, z_send, z_recv, b_send, b_recv, own_sem, s_sem, c_sem, p_send, p_recv):
    r = lax.axis_index("row")
    c = lax.axis_index("col")
    p = lax.axis_index("rep")
    ri, nu, lam = m_ref.shape
    share = ri // rows
    half = lam // 2

    barrier = pltpu.get_barrier_semaphore()
    peers = [{"row": lax.rem(r + off, rows), "rep": lax.rem(p + q, 2)} for off in range(rows) for q in range(2)]
    for peer in peers[1:] + [{"col": 1 - c}]:
        pl.semaphore_signal(barrier, inc=1, device_id=peer, device_id_type=MESH)
    pl.semaphore_wait(barrier, 2 * rows)

    def remote(src, dst, send, recv, to):
        return pltpu.make_async_remote_copy(
            src_ref=src, dst_ref=dst, send_sem=send, recv_sem=recv, device_id=to, device_id_type=MESH)

    sib_copies = []
    for g in range(ri // GROUP):
        part = pl.ds(g * GROUP, GROUP)
        sib_copies.append(remote(m_ref.at[part], sib.at[part], s_sem.at[0, g], s_sem.at[1, g], {"rep": 1 - p}))
    first = []
    for k in range(2):
        lanes = pl.ds(k * half, half)
        copies = []
        for off in range(1, rows):
            to = lax.rem(r + off, rows)
            copies.append(remote(
                m_ref.at[pl.ds(to * share, share), :, lanes],
                relaid.at[:, pl.ds(r * nu, nu), lanes],
                z_send.at[k, off], z_recv.at[k, off], {"row": to}))
        copies.append(pltpu.make_async_copy(
            m_ref.at[pl.ds(r * share, share), :, lanes],
            relaid.at[:, pl.ds(r * nu, nu), lanes], own_sem.at[0, k]))
        first.append(copies)
    for copies in first:
        for copy in copies:
            copy.start()
    for copy in sib_copies:
        copy.start()

    far_copies = []
    for g in range(ri // GROUP):
        sib_copies[g].wait()
        part = pl.ds(g * GROUP, GROUP)

        @pl.loop(0, nu // GROUP)
        def _(t):
            strip = pl.ds(pl.multiple_of(t * GROUP, GROUP), GROUP)
            mine = m_ref[part, strip, :].reshape(GROUP * GROUP, lam)
            its = sib[part, strip, :].reshape(GROUP * GROUP, lam)
            here = pl.ds(pl.multiple_of(p * lam, lam), lam)
            there = pl.ds(pl.multiple_of((1 - p) * lam, lam), lam)
            prod = jnp.dot(mine, occ_ref[here, :], preferred_element_type=F32)
            prod += jnp.dot(its, occ_ref[there, :], preferred_element_type=F32)
            prod = jnp.swapaxes(prod.reshape(GROUP, GROUP, lam), 0, 1)
            occ_own[strip, part, :] = prod.astype(BF16)

        far_copies.append(remote(
            occ_own.at[:, part, :], occ_far.at[:, part, :], c_sem.at[0, g], c_sem.at[1, g], {"col": 1 - c}))
        far_copies[-1].start()

    second = []
    for k in range(2):
        lanes = pl.ds(k * half, half)
        for copy in first[k]:
            copy.wait()

        @pl.loop(0, rows * nu // STRIP)
        def _(t):
            strip = pl.ds(pl.multiple_of(t * STRIP, STRIP), STRIP)
            weights = virt_ref[strip, :]
            pieces = [jnp.dot(weights, relaid[q, :, lanes], preferred_element_type=F32) for q in range(share)]
            turned[strip, :, lanes] = jnp.swapaxes(jnp.stack(pieces, axis=0), 0, 1).astype(BF16)

        copies = []
        for off in range(1, rows):
            to = lax.rem(r + off, rows)
            copies.append(remote(
                turned.at[pl.ds(to * nu, nu), :, lanes],
                back.at[:, pl.ds(r * share, share), lanes],
                b_send.at[k, off], b_recv.at[k, off], {"row": to}))
        copies.append(pltpu.make_async_copy(
            turned.at[pl.ds(r * nu, nu), :, lanes],
            back.at[:, pl.ds(r * share, share), lanes], own_sem.at[1, k]))
        for copy in copies:
            copy.start()
        second.append(copies)
    for copy in far_copies:
        copy.wait()
    total[...] = jnp.zeros_like(total)
    base = pl.multiple_of(c * ri, ri)
    other = pl.multiple_of((1 - c) * ri, ri)
    for k in range(2):
        lanes = pl.ds(k * half, half)
        for copy in second[k]:
            copy.wait()

        @pl.loop(0, nu // 8)
        def _(t):
            acc_own = jnp.zeros((ri, ri), F32)
            acc_far = jnp.zeros((ri, ri), F32)
            for j in range(8):
                n = t * 8 + j
                q = back[n, :, lanes]
                dims = (((1,), (1,)), ((), ()))
                acc_own += lax.dot_general(occ_own[n, :, lanes], q, dims, preferred_element_type=F32)
                acc_far += lax.dot_general(occ_far[n, :, lanes], q, dims, preferred_element_type=F32)
            total[pl.ds(base, ri), :ri] += acc_own
            total[pl.ds(other, ri), :ri] += acc_far

    tile = out_ref.shape[0]
    sends = []
    for i, peer in enumerate(peers):
        if i == 0:
            continue
        index = peer["row"] * 2 + peer["rep"]
        sends.append(remote(
            total.at[pl.ds(pl.multiple_of(index * tile, tile), tile)], parts.at[i],
            p_send.at[i], p_recv.at[i], peer))
        sends[-1].start()
    acc = total[pl.ds(pl.multiple_of((r * 2 + p) * tile, tile), tile), :]
    for i, copy in enumerate(sends):
        copy.wait()
        acc += parts[i + 1]
    out_ref[...] = acc[:, :ri] * (-2.0 / NAO)


def local(rows, integrals, occ_density, virt_density, pair_mask, aux_mask):
    ri, nu, lam = integrals.shape
    masked = integrals * keep(integrals, pair_mask, aux_mask)
    groups = ri // GROUP
    share = ri // rows
    tile = 2 * ri // (2 * rows)
    whole = pl.BlockSpec(memory_space=pltpu.VMEM)
    dma = pltpu.SemaphoreType.DMA
    return pl.pallas_call(
        functools.partial(kernel, rows),
        out_shape=jax.ShapeDtypeStruct((tile, ri), F32),
        in_specs=[whole] * 3,
        out_specs=whole,
        scratch_shapes=[
            pltpu.VMEM((ri, nu, lam), BF16),
            pltpu.VMEM((share, rows * nu, lam), BF16),
            pltpu.VMEM((rows * nu, share, lam), BF16),
            pltpu.VMEM((nu, ri, lam), BF16),
            pltpu.VMEM((nu, ri, lam), BF16),
            pltpu.VMEM((nu, ri, lam), BF16),
            pltpu.VMEM((2 * ri, 128), F32),
            pltpu.VMEM((2 * rows, tile, 128), F32),
            dma((2, rows)), dma((2, rows)), dma((2, rows)), dma((2, rows)), dma((2, 2)),
            dma((2, groups)), dma((2, groups)), dma((2 * rows,)), dma((2 * rows,)),
        ],
        compiler_params=pltpu.CompilerParams(
            collective_id=0, has_side_effects=True, vmem_limit_bytes=56 * 2**20),
    )(masked, occ_density, jnp.transpose(virt_density))


def keep(integrals, pair_mask, aux_mask):
    ri_count, nu_count, mu_count = integrals.shape
    ao_groups = pair_mask.shape[0]
    ri_groups = aux_mask.shape[0]
    pick_nu = one_hot_blocks(lax.axis_index("row") * nu_count, nu_count, BLOCK, ao_groups)
    pick_mu = one_hot_blocks(lax.axis_index("rep") * mu_count, mu_count, BLOCK, ao_groups)
    pick_ri = one_hot_blocks(lax.axis_index("col") * ri_count, ri_count, RI_ATOM, ri_groups)
    pair_float = pair_mask.astype(F32)
    aux_float = aux_mask.astype(F32)
    local_pair = jnp.dot(jnp.dot(pick_nu, jnp.transpose(pair_float)), jnp.transpose(pick_mu))
    local_aux = jnp.dot(jnp.dot(pick_ri, aux_float), jnp.transpose(pick_nu))
    return (local_aux[:, :, None] * local_pair[None, :, :]).astype(BF16)


def local_any(integrals, occ_density, virt_density, pair_mask, aux_mask):
    ri_count, nu_count, mu_count = integrals.shape
    ao_groups = pair_mask.shape[0]
    ri_groups = aux_mask.shape[0]
    pick_nu = one_hot_blocks(lax.axis_index("row") * nu_count, nu_count, BLOCK, ao_groups)
    pick_mu = one_hot_blocks(lax.axis_index("rep") * mu_count, mu_count, BLOCK, ao_groups)
    pick_ri = one_hot_blocks(lax.axis_index("col") * ri_count, ri_count, RI_ATOM, ri_groups)
    pair_float = pair_mask.astype(jnp.float32)
    aux_float = aux_mask.astype(jnp.float32)
    local_pair = jnp.dot(jnp.dot(pick_nu, jnp.transpose(pair_float)), jnp.transpose(pick_mu))
    local_aux = jnp.dot(jnp.dot(pick_ri, aux_float), jnp.transpose(pick_nu))
    keep_mask = (local_aux[:, :, None] * local_pair[None, :, :]).astype(jnp.bfloat16)
    masked = integrals * keep_mask
    lam_count = occ_density.shape[1]
    initial = jnp.zeros((ri_count, nu_count, lam_count), jnp.float32)
    block_piece = lax.all_gather(masked, "rep", axis=2, tiled=True)
    width_here = block_piece.shape[2]
    flattened = block_piece.reshape(ri_count * nu_count, width_here)
    occ_sum = jnp.dot(flattened, occ_density, preferred_element_type=jnp.float32).reshape(
        initial.shape
    )
    occ_side = occ_sum.astype(jnp.bfloat16)
    relaid = lax.all_to_all(masked, "row", split_axis=0, concat_axis=1, tiled=True)
    virt_side = jnp.einsum(
        "qsl,sn->qnl", relaid, virt_density, preferred_element_type=jnp.float32
    ).astype(jnp.bfloat16)
    virt_back = lax.all_to_all(virt_side, "row", split_axis=1, concat_axis=0, tiled=True)
    virt_flat = virt_back.reshape(ri_count, nu_count * lam_count)
    block_piece = lax.all_gather(occ_side, "col", axis=0, tiled=True)
    occ_flat = block_piece.reshape(block_piece.shape[0], nu_count * lam_count)
    partials = lax.dot_general(
        occ_flat, virt_flat, (((1,), (1,)), ((), ())), preferred_element_type=jnp.float32
    )
    summed = lax.psum_scatter(partials, ("row", "rep"), scatter_dimension=0, tiled=True)
    return summed * (-2.0 / NAO)


def solution(mesh):
    rows, cols, reps = mesh.shape["row"], mesh.shape["col"], mesh.shape["rep"]

    def run(*args):
        ri, nu, lam = args[0].shape
        if cols == 2 and reps == 2 and ri == GROUP * rows and nu % 128 == 0 and lam == 256:
            return local(rows, *args)
        return local_any(*args)

    return jax.shard_map(
        run,
        mesh=mesh,
        in_specs=(
            P(("grp", "col"), "row", "rep"),
            P("grp", "rep"),
            P("grp", None),
            P("grp", None),
            P("grp", None),
        ),
        out_specs=P(("grp", "row", "rep"), "col"),
        check_vma=False,
    )
```

```python
import jax
import jax.numpy as jnp
from jax import lax
from jax.experimental import pallas as pl
from jax.experimental.pallas import tpu as pltpu
from jax.sharding import PartitionSpec as P

BLOCK = 128
RI_ATOM = 128
NAO = 512
MESH = pl.DeviceIdType.MESH
F32 = jnp.float32
BF16 = jnp.bfloat16
GROUP = 16
STRIP = 64


def one_hot_blocks(first, count, width, groups):
    places = (first + jnp.arange(count, dtype=jnp.int32)) // width
    return (places[:, None] == jnp.arange(groups, dtype=jnp.int32)[None, :]).astype(F32)


def kernel(m_ref, occ_ref, wa_ref, wb_ref, out_ref, sib, far, far_sib, g_p, g_q, rel_a, rel_b, rel_n, occ_s, n_s,
           w, total, cross, parts, z_send, z_recv, y_send, y_recv, s_sem, x_sem, f_sem, c_sem, p_send, p_recv):
    r = lax.axis_index("row")
    c = lax.axis_index("col")
    p = lax.axis_index("rep")
    rows = 4
    ri, nu, lam = m_ref.shape
    half = lam // 2
    groups = ri // GROUP
    dims = (((1,), (1,)), ((), ()))
    lanes_of = (pl.ds(0, half), pl.ds(half, half))

    barrier = pltpu.get_barrier_semaphore()
    peers = [{"row": lax.rem(r + off, rows), "rep": lax.rem(p + q, 2)} for off in range(rows) for q in range(2)]
    for peer in peers[1:] + [{"col": 1 - c}]:
        pl.semaphore_signal(barrier, inc=1, device_id=peer, device_id_type=MESH)
    pl.semaphore_wait(barrier, 2 * rows)

    def remote(src, dst, send, recv, to):
        return pltpu.make_async_remote_copy(
            src_ref=src, dst_ref=dst, send_sem=send, recv_sem=recv, device_id=to, device_id_type=MESH)

    def part(g):
        return pl.ds(g * GROUP, GROUP)

    def slot(f):
        return pl.ds(f * nu, nu)

    sources = (3, 2, 0)

    def raw(f, blk, g, from_own):
        dst = (rel_a, rel_b)[blk].at[part(g), slot(f), :]
        src = m_ref.at[part(g), :, lanes_of[blk]] if from_own else dst
        to = lax.rem(r + (1 if f == 2 else 3), rows)
        return remote(src, dst, z_send.at[f, blk, g], z_recv.at[f, blk, g], {"row": to})

    def in_use(f, blk):
        return p == 0 if blk and f < 2 else p >= 0

    def raw_start(f, g):
        for blk in range(2):
            @pl.when((r == sources[f]) & in_use(f, blk))
            def _():
                raw(f, blk, g, True).start()

    def raw_relay(f, g, at, onward):
        for blk in range(2):
            @pl.when((r == at) & in_use(f, blk))
            def _():
                copy = raw(f, blk, g, False)
                copy.wait_recv()
                if onward:
                    copy.start()

    def right(f, arr, g, from_own):
        dst = (rel_b, rel_n)[arr].at[part(g), slot(f), :]
        src = (occ_s, n_s)[arr].at[part(g)] if from_own else dst
        return remote(src, dst, y_send.at[f, arr, g], y_recv.at[f, arr, g], {"row": lax.rem(r + 1, rows)})

    def right_start(g):
        for f in range(3):
            @pl.when((r == f) & (p == 1))
            def _():
                for arr in range(2):
                    right(f, arr, g, True).start()

    def right_relay(f, g, at):
        @pl.when((r == at) & (p == 1))
        def _():
            for arr in range(2):
                copy = right(f, arr, g, False)
                copy.wait_recv()
                if at < 3:
                    copy.start()

    sib_copies = [remote(m_ref.at[part(g)], sib.at[part(g)], s_sem.at[0, g], s_sem.at[1, g], {"rep": 1 - p})
                  for g in range(groups)]
    far_copies = [remote(m_ref.at[part(g)], far.at[part(g)], x_sem.at[0, g], x_sem.at[1, g], {"col": 1 - c})
                  for g in range(groups)]
    on_copies = [remote(far.at[part(g)], far_sib.at[part(g)], f_sem.at[0, g], f_sem.at[1, g], {"rep": 1 - p})
                 for g in range(groups)]
    for g in range(groups):
        sib_copies[g].start()
        for f in range(3):
            raw_start(f, g)
        far_copies[g].start()

    def clear(ref, f):
        @pl.loop(0, ri)
        def _(q):
            ref[q, slot(f), :] = jnp.zeros((nu, half), BF16)

    for f, at in ((0, (3,)), (1, (2, 3)), (2, (0, 2, 3))):
        for row in at:
            @pl.when(r == row)
            def _():
                clear(rel_a, f)

            @pl.when((r == row) & (p == 0))
            def _():
                clear(rel_b, f)
    for f in range(3):
        @pl.when((r <= f) & (p == 1))
        def _():
            clear(rel_n, f)

        @pl.when(((r < f) if f < 2 else (r == 0)) & (p == 1))
        def _():
            clear(rel_b, f)

        @pl.when((r == f) & (p == 1))
        def _():
            clear(rel_b, f)

    here = pl.ds(pl.multiple_of(p * lam, lam), lam)
    there = pl.ds(pl.multiple_of((1 - p) * lam, lam), lam)

    def products(x, y, g, own):
        @pl.loop(0, nu // GROUP)
        def _(t):
            strip = pl.ds(pl.multiple_of(t * GROUP, GROUP), GROUP)
            mine = x[part(g), strip, :]
            its = y[part(g), strip, :].reshape(GROUP * GROUP, lam)
            prod = jnp.dot(mine.reshape(GROUP * GROUP, lam), occ_ref[here, :], preferred_element_type=F32)
            prod += jnp.dot(its, occ_ref[there, :], preferred_element_type=F32)
            prod = prod.reshape(GROUP, GROUP, 2 * lam)
            turned = jnp.swapaxes(prod, 0, 1).astype(BF16)
            to = pl.ds(g * GROUP + (0 if own else ri), GROUP)
            g_p[strip, to, :] = turned[:, :, :lam]
            g_q[strip, to, :] = turned[:, :, lam:]

            @pl.when((p == 1) & (r != 1))
            def _():
                plain = jnp.swapaxes(mine[:, :, half:].astype(F32), 0, 1).astype(BF16)
                g_p[strip, to, half:] = plain
                g_q[strip, to, half:] = plain

            @pl.when(p == 1)
            def _():
                if own:
                    occ_s[part(g), strip, :] = prod[:, :, half:lam].astype(BF16)
                    n_s[part(g), strip, :] = prod[:, :, lam + half:].astype(BF16)

    for g in range(groups):
        sib_copies[g].wait()
        products(m_ref, sib, g, True)
        right_start(g)
        raw_relay(0, g, 2, True)
        raw_relay(1, g, 1, True)
    for g in range(groups):
        right_relay(0, g, 1)
        right_relay(1, g, 2)
        raw_relay(0, g, 1, True)
        right_relay(2, g, 3)
        far_copies[g].wait()
        on_copies[g].start()
        right_relay(0, g, 2)
        raw_relay(2, g, 1, False)
        if g:
            on_copies[g - 1].wait()
            products(far, far_sib, g - 1, False)
    on_copies[groups - 1].wait()
    products(far, far_sib, groups - 1, False)

    def mixed(g, blk):
        rel, w_ref = (rel_a, rel_b)[blk], (wa_ref, wb_ref)[blk]

        def strips(first, last, moved, own):
            @pl.loop(first // STRIP, last // STRIP)
            def _(t):
                strip = pl.ds(pl.multiple_of(t * STRIP, STRIP), STRIP)
                pieces = []
                for q in range(g * GROUP, (g + 1) * GROUP):
                    piece = jnp.dot(w_ref[strip, :3 * nu], moved[q], preferred_element_type=F32)
                    if own is not None:
                        piece += jnp.dot(w_ref[strip, 3 * nu:], own(q), preferred_element_type=F32)
                    pieces.append(piece)
                w[strip, part(g), :] = jnp.swapaxes(jnp.stack(pieces, axis=0), 0, 1).astype(BF16)

        def raw_own(q):
            return m_ref[q, :, lanes_of[blk]]

        if blk == 0:
            strips(0, nu, rel, raw_own)
            strips(nu, 2 * nu, rel, None)
            return

        @pl.when(p == 0)
        def _():
            strips(0, nu, rel, raw_own)
            strips(nu, 2 * nu, rel, None)

        @pl.when(p == 1)
        def _():
            strips(0, nu, rel_n, None)
            strips(nu, 2 * nu, rel, lambda q: occ_s[q])

    def grams(blk):
        lanes = lanes_of[blk]

        @pl.loop(0, nu // 8)
        def _(t):
            acc_p = jnp.zeros((2 * ri, ri), F32)
            acc_q = jnp.zeros((ri, 2 * ri), F32)
            for j in range(8):
                n = t * 8 + j
                acc_p += lax.dot_general(g_p[n, :, lanes], w[n], dims, preferred_element_type=F32)
                acc_q += lax.dot_general(w[nu + n], g_q[n, :, lanes], dims, preferred_element_type=F32)
            total[pl.ds(base, ri), :ri] += acc_p[:ri] + acc_q[:, :ri]
            total[pl.ds(other, ri), :ri] += acc_p[ri:]
            cross[0, :, :ri] += acc_q[:, ri:]

    base = pl.multiple_of(c * ri, ri)
    other = pl.multiple_of((1 - c) * ri, ri)
    total[...] = jnp.zeros_like(total)
    cross[0] = jnp.zeros((ri, 2 * ri), F32)

    @pl.when((r == 1) & (p == 1))
    def _():
        for g in range(groups):
            @pl.loop(0, 2 * nu // STRIP)
            def _(t):
                strip = pl.ds(pl.multiple_of(t * STRIP, STRIP), STRIP)
                pieces = [jnp.dot(wa_ref[strip, 2 * nu:3 * nu], rel_b[q, slot(2), :], preferred_element_type=F32)
                          for q in range(g * GROUP, (g + 1) * GROUP)]
                w[strip, part(g), :] = jnp.swapaxes(jnp.stack(pieces, axis=0), 0, 1).astype(BF16)
        grams(1)
        for x, shift in ((m_ref, 0), (far, ri)):
            for g in range(groups):
                @pl.loop(0, nu // GROUP)
                def _(t):
                    strip = pl.ds(pl.multiple_of(t * GROUP, GROUP), GROUP)
                    to = pl.ds(g * GROUP + shift, GROUP)
                    plain = jnp.swapaxes(x[part(g), strip, half:].astype(F32), 0, 1).astype(BF16)
                    g_p[strip, to, half:] = plain
                    g_q[strip, to, half:] = plain

    for g in range(groups):
        raw_relay(0, g, 0, False)
        raw_relay(1, g, 0, False)
        right_relay(1, g, 3)
        right_relay(0, g, 3)
        mixed(g, 0)
    grams(0)
    for g in range(groups):
        mixed(g, 1)
    grams(1)

    copy = remote(cross.at[0], cross.at[1], c_sem.at[0], c_sem.at[1], {"col": 1 - c})
    copy.start()
    copy.wait()
    total[pl.ds(other, ri), :] += cross[1]

    tile = out_ref.shape[0]
    sends = []
    for i, peer in enumerate(peers):
        if i == 0:
            continue
        index = peer["row"] * 2 + peer["rep"]
        sends.append(remote(
            total.at[pl.ds(pl.multiple_of(index * tile, tile), tile)], parts.at[i],
            p_send.at[i], p_recv.at[i], peer))
        sends[-1].start()
    for g in range(groups):
        for f, senders in enumerate(((1, 2, 3), (1, 2), (0,))):
            for row in senders:
                for blk in range(2):
                    @pl.when((r == row) & in_use(f, blk))
                    def _():
                        raw(f, blk, g, row == sources[f]).wait_send()
        for f in range(3):
            for row in range(f, 3):
                @pl.when((r == row) & (p == 1))
                def _():
                    for arr in range(2):
                        right(f, arr, g, row == f).wait_send()
    acc = total[pl.ds(pl.multiple_of((r * 2 + p) * tile, tile), tile), :]
    for i, copy in enumerate(sends):
        copy.wait()
        acc += parts[i + 1]
    out_ref[...] = acc[:, :ri] * (-2.0 / NAO)


def local(rows, integrals, occ_density, virt_density, pair_mask, aux_mask):
    ri, nu, lam = integrals.shape
    r, p = lax.axis_index("row"), lax.axis_index("rep")
    masked = integrals * keep(integrals, pair_mask, aux_mask)
    groups = ri // GROUP
    tile = 2 * ri // (2 * rows)
    half = lam // 2
    occ_all = lax.all_gather(occ_density, "rep", axis=1, tiled=True)
    occ_w = jnp.concatenate(
        [occ_density, jnp.transpose(lax.dynamic_slice_in_dim(occ_all, p * lam, lam, 0))], axis=1)
    column = jnp.transpose(lax.dynamic_slice_in_dim(virt_density, r * nu, nu, 1))
    row = lax.dynamic_slice_in_dim(virt_density, r * nu, nu, 0)
    both = jnp.concatenate([column, row], axis=0)

    def block(src):
        return both[:, src * nu:(src + 1) * nu]

    own = lax.dynamic_slice_in_dim(both, r * nu, nu, 1)
    zero = jnp.zeros_like(own)
    upper = jnp.concatenate([own[:nu], zero[:nu]])
    lower = jnp.concatenate([zero[:nu], own[nu:]])
    wa = jnp.concatenate(
        [jnp.where(r <= 2, block(3), 0), jnp.where(r <= 1, block(2), 0), jnp.where(r == 1, block(0), 0), upper], axis=1)
    wc = jnp.concatenate([jnp.where((f < r) & ((f > 0) | (r > 1)), block(f), 0) for f in range(3)] + [lower], axis=1)
    wb = jnp.where(p == 0, wa, wc)
    whole = pl.BlockSpec(memory_space=pltpu.VMEM)
    dma = pltpu.SemaphoreType.DMA
    return pl.pallas_call(
        kernel,
        out_shape=jax.ShapeDtypeStruct((tile, ri), F32),
        in_specs=[whole] * 4,
        out_specs=whole,
        scratch_shapes=[
            pltpu.VMEM((ri, nu, lam), BF16),
            pltpu.VMEM((ri, nu, lam), BF16),
            pltpu.VMEM((ri, nu, lam), BF16),
            pltpu.VMEM((nu, 2 * ri, lam), BF16),
            pltpu.VMEM((nu, 2 * ri, lam), BF16),
            pltpu.VMEM((ri, 3 * nu, half), BF16),
            pltpu.VMEM((ri, 3 * nu, half), BF16),
            pltpu.VMEM((ri, 3 * nu, half), BF16),
            pltpu.VMEM((ri, nu, half), BF16),
            pltpu.VMEM((ri, nu, half), BF16),
            pltpu.VMEM((2 * nu, ri, half), BF16),
            pltpu.VMEM((2 * ri, 2 * ri), F32),
            pltpu.VMEM((2, ri, 2 * ri), F32),
            pltpu.VMEM((2 * rows, tile, 2 * ri), F32),
            dma((3, 2, groups)), dma((3, 2, groups)), dma((3, 2, groups)), dma((3, 2, groups)),
            dma((2, groups)), dma((2, groups)), dma((2, groups)), dma((2,)),
            dma((2 * rows,)), dma((2 * rows,)),
        ],
        compiler_params=pltpu.CompilerParams(
            collective_id=0, has_side_effects=True, vmem_limit_bytes=62 * 2**20),
    )(masked, occ_w, wa, wb)


def keep(integrals, pair_mask, aux_mask):
    ri_count, nu_count, mu_count = integrals.shape
    ao_groups = pair_mask.shape[0]
    ri_groups = aux_mask.shape[0]
    pick_nu = one_hot_blocks(lax.axis_index("row") * nu_count, nu_count, BLOCK, ao_groups)
    pick_mu = one_hot_blocks(lax.axis_index("rep") * mu_count, mu_count, BLOCK, ao_groups)
    pick_ri = one_hot_blocks(lax.axis_index("col") * ri_count, ri_count, RI_ATOM, ri_groups)
    pair_float = pair_mask.astype(F32)
    aux_float = aux_mask.astype(F32)
    local_pair = jnp.dot(jnp.dot(pick_nu, jnp.transpose(pair_float)), jnp.transpose(pick_mu))
    local_aux = jnp.dot(jnp.dot(pick_ri, aux_float), jnp.transpose(pick_nu))
    return (local_aux[:, :, None] * local_pair[None, :, :]).astype(BF16)


def local_any(integrals, occ_density, virt_density, pair_mask, aux_mask):
    ri_count, nu_count, mu_count = integrals.shape
    ao_groups = pair_mask.shape[0]
    ri_groups = aux_mask.shape[0]
    pick_nu = one_hot_blocks(lax.axis_index("row") * nu_count, nu_count, BLOCK, ao_groups)
    pick_mu = one_hot_blocks(lax.axis_index("rep") * mu_count, mu_count, BLOCK, ao_groups)
    pick_ri = one_hot_blocks(lax.axis_index("col") * ri_count, ri_count, RI_ATOM, ri_groups)
    pair_float = pair_mask.astype(jnp.float32)
    aux_float = aux_mask.astype(jnp.float32)
    local_pair = jnp.dot(jnp.dot(pick_nu, jnp.transpose(pair_float)), jnp.transpose(pick_mu))
    local_aux = jnp.dot(jnp.dot(pick_ri, aux_float), jnp.transpose(pick_nu))
    keep_mask = (local_aux[:, :, None] * local_pair[None, :, :]).astype(jnp.bfloat16)
    masked = integrals * keep_mask
    lam_count = occ_density.shape[1]
    initial = jnp.zeros((ri_count, nu_count, lam_count), jnp.float32)
    block_piece = lax.all_gather(masked, "rep", axis=2, tiled=True)
    width_here = block_piece.shape[2]
    flattened = block_piece.reshape(ri_count * nu_count, width_here)
    occ_sum = jnp.dot(flattened, occ_density, preferred_element_type=jnp.float32).reshape(
        initial.shape
    )
    occ_side = occ_sum.astype(jnp.bfloat16)
    relaid = lax.all_to_all(masked, "row", split_axis=0, concat_axis=1, tiled=True)
    virt_side = jnp.einsum(
        "qsl,sn->qnl", relaid, virt_density, preferred_element_type=jnp.float32
    ).astype(jnp.bfloat16)
    virt_back = lax.all_to_all(virt_side, "row", split_axis=1, concat_axis=0, tiled=True)
    virt_flat = virt_back.reshape(ri_count, nu_count * lam_count)
    block_piece = lax.all_gather(occ_side, "col", axis=0, tiled=True)
    occ_flat = block_piece.reshape(block_piece.shape[0], nu_count * lam_count)
    partials = lax.dot_general(
        occ_flat, virt_flat, (((1,), (1,)), ((), ())), preferred_element_type=jnp.float32
    )
    summed = lax.psum_scatter(partials, ("row", "rep"), scatter_dimension=0, tiled=True)
    return summed * (-2.0 / NAO)


def solution(mesh):
    rows, cols, reps = mesh.shape["row"], mesh.shape["col"], mesh.shape["rep"]

    def run(*args):
        ri, nu, lam = args[0].shape
        if rows == 4 and cols == 2 and reps == 2 and ri == 64 and nu == 128 and lam == 256:
            return local(rows, *args)
        return local_any(*args)

    return jax.shard_map(
        run,
        mesh=mesh,
        in_specs=(
            P(("grp", "col"), "row", "rep"),
            P("grp", "rep"),
            P("grp", None),
            P("grp", None),
            P("grp", None),
        ),
        out_specs=P(("grp", "row", "rep"), "col"),
        check_vma=False,
    )
```
